32 devices in a mesh: items: 2 (over y), codes: 16 (over z, x, core).
Axes of the slice: x: 2, y: 2, z: 4, core: 2. Of those that a mesh axis runs over, the one named last changes fastest.
Arguments:
- residuals: bfloat16 [512, 256], P(('items', 'codes')), may hold values from -6 to 6
- codebook: bfloat16 [4096, 256], P('codes'), may hold values from -6 to 6
Outputs:
- new_codebook: float32 [4096, 256], P('codes')
- next_residuals: float32 [512, 256], P(('items', 'codes'))
The draws below stay inside these ranges and needn't reach their ends.
All inputs are finite; a program needn't handle non-finite values.
Results may differ from the reference program's by a relative error of at most 0.0024.
Values may be sent and summed in bfloat16 or wider, within the bound.
A program may use at most 64 MiB of HBM per device.

```python
import jax
import jax.numpy as jnp
from jax import lax

D = 256
ITERS = 3
CODES = 4096
ITEMS = 512


def block_scale(key, extent, pieces, smallest, top_value):
    def one(position, shards_of):
        heights = jax.random.uniform(jax.random.fold_in(jax.random.fold_in(key, 6), position), (shards_of,), jnp.float32, smallest / len(pieces), top_value / len(pieces))
        return jnp.repeat(jnp.exp(heights), extent[position] // shards_of).reshape((-1,) + (1,) * (len(extent) - position - 1))

    loudness = one(*pieces[0])
    for cut in pieces[1:]:
        loudness = loudness * one(*cut)
    return loudness


def bell_draw(stream_key, shape, scale, limit, split=(), dtype=jnp.bfloat16):
    array = jax.random.normal(stream_key, shape, jnp.float32) * scale
    if len(split) > 0:
        array = block_scale(stream_key, shape, split, -0.22, 0.18) * array
    return jnp.clip(array, min=-limit, max=limit).astype(dtype)


def setup_inputs(seed: int = 0) -> dict:
    keys = jax.random.split(jax.random.key(seed), 3)
    return {
        "residuals": bell_draw(keys[0], (ITEMS, D), 1.0, 6.0, ((0, 32),)),
        "codebook": bell_draw(keys[1], (CODES, D), 1.0, 6.0, ((0, 16),)),
    }


EPSILON = 1e-06
SHARPNESS = 40.0

def reference(residuals, codebook):
    items_total = residuals.shape[0]
    codes_total = codebook.shape[0]
    feature_count = residuals.shape[1]
    rows_float = residuals.astype(jnp.float32)
    codes_float = codebook.astype(jnp.float32)
    row_scale = lax.rsqrt(lax.optimization_barrier(jnp.mean(rows_float * rows_float, axis=1)) + EPSILON)
    code_scale = lax.rsqrt(lax.optimization_barrier(jnp.mean(codes_float * codes_float, axis=1)) + EPSILON)
    block_rows = min(4096, items_total)
    block_count = items_total // block_rows
    row_blocks = residuals.reshape(block_count, block_rows, feature_count)
    scale_blocks = row_scale.reshape(block_count, block_rows)

    def kernel_block(inputs):
        block, scales = inputs
        similarity = lax.dot_general(block, codebook, (((1,), (1,)), ((), ())), preferred_element_type=jnp.float32)
        return jnp.exp(SHARPNESS * similarity * scales[:, None] * code_scale[None, :] / feature_count)
    kernel = lax.map(kernel_block, (row_blocks, scale_blocks))
    balance = items_total / codes_total
    weights_rows = jnp.ones((block_count, block_rows), jnp.float32)
    weights_cols = jnp.ones((codes_total,), jnp.float32)
    for sweep in range(ITERS):
        column_total = jnp.einsum('bn,bnk->k', weights_rows, kernel, precision=lax.Precision.HIGHEST)
        weights_cols = balance / column_total
        row_total = jnp.einsum('bnk,k->bn', kernel, weights_cols, precision=lax.Precision.HIGHEST)
        weights_rows = 1.0 / row_total

    def finish(totals, inputs):
        kernel_rows, row_weights, block = inputs
        numerator, mass = totals
        transport = (kernel_rows * row_weights[:, None] * weights_cols[None, :]).astype(jnp.bfloat16)
        numerator = numerator + lax.dot_general(transport, block, (((0,), (0,)), ((), ())), preferred_element_type=jnp.float32)
        mass = mass + lax.optimization_barrier(jnp.sum(transport.astype(jnp.float32), axis=0))
        rebuilt = jnp.dot(transport, codebook, preferred_element_type=jnp.float32)
        return ((numerator, mass), block.astype(jnp.float32) - rebuilt)
    start_totals = (jnp.zeros((codes_total, feature_count), jnp.float32), jnp.zeros((codes_total,), jnp.float32))
    (numerator, mass), following = lax.scan(finish, start_totals, (kernel, weights_rows, row_blocks))
    return (numerator / mass[:, None], following.reshape(items_total, feature_count))
```

```python
import functools
import math

import jax
import jax.numpy as jnp
from jax import lax
from jax.experimental import pallas as pl
from jax.experimental.pallas import tpu as pltpu
from jax.sharding import PartitionSpec as P

ITERS = 3
EPSILON = 1e-06
SHARPNESS = 40.0
PART = jnp.bfloat16
MESH = pl.DeviceIdType.MESH
NT = (((1,), (1,)), ((), ()))
TN = (((0,), (0,)), ((), ()))


def drain(ref, sem):
    pltpu.make_async_copy(ref, ref, sem).wait()


def each(count, body):
    if count <= 32:
        for i in range(count):
            body(i)
    else:
        pl.loop(0, count)(body)


def kernel(
    groups, shards, cores,
    res_ref, code_ref, newc_ref, next_ref,
    items_ref, kern_ref, u_ref, row_out, row_in, part_out, part_in,
    gather_send, gather_recv, pair_send, pair_recv, row_send, row_recv, part_send, part_recv,
):
    f32, bf16 = jnp.float32, jnp.bfloat16
    y, c = lax.axis_index("items"), lax.axis_index("codes")
    rows, features = res_ref.shape
    codes = code_ref.shape[0]
    devices = groups * shards
    items = devices * rows
    line = shards // cores
    half = line * rows
    core, chip = lax.rem(c, cores), lax.div(c, cores)

    def start_of(group, lane):
        return pl.multiple_of((group * cores + lane) * half, half)

    barrier = pltpu.get_barrier_semaphore()
    me = y * shards + c

    def greet(i):
        other = lax.rem(me + i + 1, devices)
        pl.semaphore_signal(
            barrier, inc=1,
            device_id=(lax.div(other, shards), lax.rem(other, shards)), device_id_type=MESH,
        )

    each(devices - 1, greet)

    mine = pl.ds(pl.multiple_of((y * cores + core) * half + chip * rows, rows), rows)
    items_ref[mine, :] = res_ref[...]
    code = code_ref[...]
    code32 = code.astype(f32)
    code_scale = lax.rsqrt(jnp.sum(code32 * code32, axis=1, keepdims=True) / features + EPSILON)
    code_scale = code_scale * (SHARPNESS * math.log2(math.e) / features)
    pl.semaphore_wait(barrier, devices - 1)

    spot = y * line + chip
    chips = groups * line

    def spread(i):
        other = lax.rem(spot + i + 1, chips)
        pltpu.make_async_remote_copy(
            src_ref=res_ref, dst_ref=items_ref.at[mine],
            send_sem=gather_send, recv_sem=gather_recv,
            device_id=(lax.div(other, line), lax.rem(other, line) * cores + core),
            device_id_type=MESH,
        ).start()

    each(chips - 1, spread)
    drain(items_ref.at[pl.ds(0, (chips - 1) * rows)], gather_recv)
    if cores == 2:
        for g in range(groups):
            block = items_ref.at[pl.ds(start_of(g, core), half)]
            pltpu.make_async_remote_copy(
                src_ref=block, dst_ref=block, send_sem=pair_send, recv_sem=pair_recv,
                device_id=(y, c + 1 - 2 * core), device_id_type=MESH,
            ).start()

    ones = jnp.ones((16, features), bf16)

    def build(start):
        block = items_ref[pl.ds(start, half), :]
        sim = lax.dot_general(code, block, NT, preferred_element_type=f32)
        wide = block.astype(f32)
        square = wide * wide
        high = square.astype(bf16)
        low = (square - high.astype(f32)).astype(bf16)
        mean = lax.dot_general(ones, high, NT, preferred_element_type=f32)
        mean = mean + lax.dot_general(ones, low, NT, preferred_element_type=f32)
        row_scale = lax.rsqrt(mean[0:1] / features + EPSILON)
        kern_ref[:, pl.ds(start, half)] = jnp.exp2(sim * code_scale * row_scale)

    each(groups, lambda g: build(start_of(g, core)))
    if cores == 2:
        drain(items_ref.at[pl.ds(0, chips * rows)], pair_recv)
        each(groups, lambda g: build(start_of(g, 1 - core)))

    width = math.gcd(items, 512)
    pieces = items // width

    def lanes(i):
        if pieces == 1:
            return pl.ds(0, width)
        return pl.ds(pl.multiple_of(i * width, width), width)

    def over_pieces(body, carry):
        if pieces == 1:
            return body(0, carry)
        return lax.fori_loop(0, pieces, body, carry)

    balance = items / (codes * shards)

    def column_sum(first):
        def body(i, total):
            k = kern_ref[:, lanes(i)]
            if not first:
                k = k * u_ref[:, lanes(i)]
            return total + jnp.sum(k, axis=1, keepdims=True)
        return over_pieces(body, jnp.zeros((codes, 1), f32))

    def row_sum(sweep, v):
        def body(i, none):
            row_out[sweep, :, lanes(i)] = jnp.sum(kern_ref[:, lanes(i)] * v, axis=0, keepdims=True)
            return none
        over_pieces(body, 0)

    def send_rows(sweep):
        def one(j):
            pltpu.make_async_remote_copy(
                src_ref=row_out.at[sweep], dst_ref=row_in.at[sweep, j],
                send_sem=row_send.at[sweep], recv_sem=row_recv.at[sweep],
                device_id=(y, lax.rem(c + j + 1, shards)), device_id_type=MESH,
            ).start()
        each(shards - 1, one)

    def finish_rows(sweep):
        drain(row_in.at[sweep], row_recv.at[sweep])

        def body(i, none):
            total = row_out[sweep, :, lanes(i)]
            if shards <= 32:
                for j in range(shards - 1):
                    total = total + row_in[sweep, j, :, lanes(i)]
            else:
                total = lax.fori_loop(
                    0, shards - 1, lambda j, t: t + row_in[sweep, j, :, lanes(i)], total
                )
            u_ref[:, lanes(i)] = 1.0 / total
            return none
        over_pieces(body, 0)

    for sweep in range(ITERS):
        v = balance / column_sum(sweep == 0)
        row_sum(sweep, v)
        send_rows(sweep)
        if sweep < ITERS - 1:
            finish_rows(sweep)

    def partial(lane):
        plan = (kern_ref[:, pl.ds(start_of(y, lane), half)] * v).astype(bf16)
        part = lax.dot_general(plan, code, TN, preferred_element_type=f32)
        part_out[pl.ds(lane * half, half), :] = part.astype(part_out.dtype)

    each(cores, partial)

    def send_part(j):
        other = lax.rem(c + j + 1, shards)
        index = lax.rem(other, cores) * line + lax.div(other, cores)
        pltpu.make_async_remote_copy(
            src_ref=part_out.at[pl.ds(pl.multiple_of(index * rows, rows), rows)],
            dst_ref=part_in.at[j],
            send_sem=part_send, recv_sem=part_recv,
            device_id=(y, other), device_id_type=MESH,
        ).start()

    each(shards - 1, send_part)

    finish_rows(ITERS - 1)

    def gather_codes(i, carry):
        numerator, mass = carry
        plan = (kern_ref[:, lanes(i)] * u_ref[:, lanes(i)] * v).astype(bf16)
        block = items_ref[lanes(i), :]
        numerator = numerator + jnp.dot(plan, block, preferred_element_type=f32)
        return numerator, mass + jnp.sum(plan.astype(f32), axis=1, keepdims=True)

    numerator, mass = over_pieces(
        gather_codes, (jnp.zeros((codes, features), f32), jnp.zeros((codes, 1), f32))
    )
    newc_ref[...] = numerator / mass

    start = (y * cores + core) * half + chip * rows
    def pick(i, total):
        lane = lax.broadcasted_iota(jnp.int32, (rows, width), 1) + i * width
        row = lax.broadcasted_iota(jnp.int32, (rows, width), 0) + start
        chosen = jnp.where(lane == row, u_ref[:, lanes(i)], 0.0)
        return total + jnp.sum(chosen, axis=1, keepdims=True)

    u_mine = over_pieces(pick, jnp.zeros((rows, 1), f32))

    drain(part_in, part_recv)
    own = pl.ds(pl.multiple_of((core * line + chip) * rows, rows), rows)
    rebuilt = part_out[own, :].astype(f32)
    if shards <= 32:
        for j in range(shards - 1):
            rebuilt = rebuilt + part_in[j].astype(f32)
    else:
        rebuilt = lax.fori_loop(
            0, shards - 1, lambda j, t: t + part_in[j].astype(f32), rebuilt
        )
    next_ref[...] = res_ref[...].astype(f32) - rebuilt * u_mine

    drain(items_ref.at[pl.ds(0, (chips - 1) * rows)], gather_send)
    if cores == 2:
        drain(items_ref.at[pl.ds(0, chips * rows)], pair_send)
    for sweep in range(ITERS):
        drain(row_in.at[sweep], row_send.at[sweep])
    drain(part_in, part_send)


def shards_of(groups, shards, residuals, codebook):
    rows, features = residuals.shape
    codes = codebook.shape[0]
    cores = 2 if shards % 2 == 0 else 1
    items = groups * shards * rows
    f32, bf16 = jnp.float32, jnp.bfloat16
    dma = pltpu.SemaphoreType.DMA
    vmem = pl.BlockSpec(memory_space=pltpu.VMEM)
    return pl.pallas_call(
        functools.partial(kernel, groups, shards, cores),
        out_shape=(
            jax.ShapeDtypeStruct((codes, features), f32),
            jax.ShapeDtypeStruct((rows, features), f32),
        ),
        in_specs=[vmem, vmem],
        out_specs=(vmem, vmem),
        scratch_shapes=[
            pltpu.VMEM((items, features), bf16),
            pltpu.VMEM((codes, items), f32),
            pltpu.VMEM((1, items), f32),
            pltpu.VMEM((ITERS, 1, items), f32),
            pltpu.VMEM((ITERS, shards - 1, 1, items), f32),
            pltpu.VMEM((shards * rows, features), PART),
            pltpu.VMEM((shards - 1, rows, features), PART),
            dma, dma, dma, dma, dma((ITERS,)), dma((ITERS,)), dma, dma,
        ],
        compiler_params=pltpu.CompilerParams(
            collective_id=0, has_side_effects=True, vmem_limit_bytes=48 * 2**20
        ),
    )(residuals, codebook)


def solution(mesh):
    groups, shards = mesh.shape["items"], mesh.shape["codes"]
    return jax.shard_map(
        functools.partial(shards_of, groups, shards),
        mesh=mesh,
        in_specs=(P(("items", "codes"), None), P("codes", None)),
        out_specs=(P("codes", None), P(("items", "codes"), None)),
        check_vma=False,
    )
```

```python
import functools
import math

import jax
import jax.numpy as jnp
from jax import lax
from jax.experimental import pallas as pl
from jax.experimental.pallas import tpu as pltpu
from jax.sharding import PartitionSpec as P

ITERS = 3
EPSILON = 1e-06
SHARPNESS = 40.0
PART = jnp.bfloat16
MESH = pl.DeviceIdType.MESH
NT = (((1,), (1,)), ((), ()))
TN = (((0,), (0,)), ((), ()))


def drain(ref, sem):
    pltpu.make_async_copy(ref, ref, sem).wait()


def each(count, body):
    if count <= 32:
        for i in range(count):
            body(i)
    else:
        pl.loop(0, count)(body)


def kernel(
    groups, shards, cores,
    res_hbm, code_hbm, newc_ref, next_ref,
    res_ref, code_ref, items_ref, kern_ref, u_ref, row_out, row_in, part_out, part_in,
    load, gather_send, gather_recv, pair_send, pair_recv, row_send, row_recv, part_send, part_recv,
):
    f32, bf16 = jnp.float32, jnp.bfloat16
    y, c = lax.axis_index("items"), lax.axis_index("codes")
    rows, features = res_ref.shape
    codes = code_ref.shape[0]
    devices = groups * shards
    items = devices * rows
    line = shards // cores
    half = line * rows
    core, chip = lax.rem(c, cores), lax.div(c, cores)

    def start_of(group, lane):
        return pl.multiple_of((group * cores + lane) * half, half)

    barrier = pltpu.get_barrier_semaphore()
    spot = y * line + chip
    chips = groups * line
    partners = chips - 1 + (line if cores == 2 else 0)

    def greet_chip(i):
        other = lax.rem(spot + i + 1, chips)
        pl.semaphore_signal(
            barrier, inc=1,
            device_id=(lax.div(other, line), lax.rem(other, line) * cores + core),
            device_id_type=MESH,
        )

    def greet_core(i):
        other = lax.rem(chip + i, line) * cores + 1 - core
        pl.semaphore_signal(barrier, inc=1, device_id=(y, other), device_id_type=MESH)

    each(chips - 1, greet_chip)
    if cores == 2:
        each(line, greet_core)
    load_res = pltpu.make_async_copy(res_hbm, res_ref, load.at[0])
    load_code = pltpu.make_async_copy(code_hbm, code_ref, load.at[1])
    load_res.start()
    load_code.start()

    load_res.wait()
    load_code.wait()
    mine = pl.ds(pl.multiple_of((y * cores + core) * half + chip * rows, rows), rows)
    items_ref[mine, :] = res_ref[...]
    code = code_ref[...]
    code32 = code.astype(f32)
    code_scale = lax.rsqrt(jnp.sum(code32 * code32, axis=1, keepdims=True) / features + EPSILON)
    code_scale = code_scale * (SHARPNESS * math.log2(math.e) / features)
    pl.semaphore_wait(barrier, partners)

    def spread(i):
        other = lax.rem(2 * chips - 1 - spot - i, chips)

        @pl.when(other != spot)
        def _():
            pltpu.make_async_remote_copy(
                src_ref=res_ref, dst_ref=items_ref.at[mine],
                send_sem=gather_send, recv_sem=gather_recv.at[y],
                device_id=(lax.div(other, line), lax.rem(other, line) * cores + core),
                device_id_type=MESH,
            ).start()

    each(chips, spread)
    for i in range(groups):
        g = lax.rem(y + i, groups)
        arrive = (line - 1 if i == 0 else line) * rows
        if arrive:
            drain(items_ref.at[pl.ds(0, arrive)], gather_recv.at[g])
        if cores == 2:
            block = items_ref.at[pl.ds(start_of(g, core), half)]
            pltpu.make_async_remote_copy(
                src_ref=block, dst_ref=block, send_sem=pair_send, recv_sem=pair_recv,
                device_id=(y, c + 1 - 2 * core), device_id_type=MESH,
            ).start()

    ones = jnp.ones((16, features), bf16)

    def build(start):
        block = items_ref[pl.ds(start, half), :]
        sim = lax.dot_general(code, block, NT, preferred_element_type=f32)
        wide = block.astype(f32)
        square = wide * wide
        high = square.astype(bf16)
        low = (square - high.astype(f32)).astype(bf16)
        mean = lax.dot_general(ones, high, NT, preferred_element_type=f32)
        mean = mean + lax.dot_general(ones, low, NT, preferred_element_type=f32)
        row_scale = lax.rsqrt(mean[0:1] / features + EPSILON)
        kern_ref[:, pl.ds(start, half)] = jnp.exp2(sim * code_scale * row_scale)

    each(groups, lambda g: build(start_of(g, core)))
    if cores == 2:
        drain(items_ref.at[pl.ds(0, chips * rows)], pair_recv)
        each(groups, lambda g: build(start_of(g, 1 - core)))

    width = math.gcd(items, 512)
    pieces = items // width

    def lanes(i):
        if pieces == 1:
            return pl.ds(0, width)
        return pl.ds(pl.multiple_of(i * width, width), width)

    def over_pieces(body, carry):
        if pieces == 1:
            return body(0, carry)
        return lax.fori_loop(0, pieces, body, carry)

    balance = items / (codes * shards)

    def column_sum(first):
        def body(i, total):
            k = kern_ref[:, lanes(i)]
            if not first:
                k = k * u_ref[:, lanes(i)]
            return total + jnp.sum(k, axis=1, keepdims=True)
        return over_pieces(body, jnp.zeros((codes, 1), f32))

    def row_sum(sweep, v):
        def body(i, none):
            row_out[sweep, :, lanes(i)] = jnp.sum(kern_ref[:, lanes(i)] * v, axis=0, keepdims=True)
            return none
        over_pieces(body, 0)

    def send_rows(sweep):
        def one(j):
            other = lax.rem(2 * shards - 1 - c - j, shards)

            @pl.when(other != c)
            def _():
                pltpu.make_async_remote_copy(
                    src_ref=row_out.at[sweep], dst_ref=row_in.at[sweep, c],
                    send_sem=row_send.at[sweep], recv_sem=row_recv.at[sweep],
                    device_id=(y, other), device_id_type=MESH,
                ).start()
        each(shards, one)

    def finish_rows(sweep):
        drain(row_in.at[sweep, pl.ds(0, shards - 1)], row_recv.at[sweep])
        row_in[sweep, c] = row_out[sweep]

        def body(i, none):
            total = jnp.zeros((1, width), f32)
            if shards <= 32:
                for j in range(shards):
                    total = total + row_in[sweep, j, :, lanes(i)]
            else:
                total = lax.fori_loop(
                    0, shards, lambda j, t: t + row_in[sweep, j, :, lanes(i)], total
                )
            u_ref[:, lanes(i)] = 1.0 / total
            return none
        over_pieces(body, 0)

    for sweep in range(ITERS):
        v = balance / column_sum(sweep == 0)
        row_sum(sweep, v)
        send_rows(sweep)
        if sweep < ITERS - 1:
            finish_rows(sweep)

    def partial(lane):
        plan = (kern_ref[:, pl.ds(start_of(y, lane), half)] * v).astype(bf16)
        part = lax.dot_general(plan, code, TN, preferred_element_type=f32)
        part_out[pl.ds(lane * half, half), :] = part.astype(part_out.dtype)

    each(cores, partial)

    def send_part(j):
        other = lax.rem(2 * shards - 1 - c - j, shards)
        index = lax.rem(other, cores) * line + lax.div(other, cores)

        @pl.when(other != c)
        def _():
            pltpu.make_async_remote_copy(
                src_ref=part_out.at[pl.ds(pl.multiple_of(index * rows, rows), rows)],
                dst_ref=part_in.at[c],
                send_sem=part_send, recv_sem=part_recv,
                device_id=(y, other), device_id_type=MESH,
            ).start()

    each(shards, send_part)

    finish_rows(ITERS - 1)

    def gather_codes(i, carry):
        numerator, mass = carry
        plan = (kern_ref[:, lanes(i)] * u_ref[:, lanes(i)] * v).astype(bf16)
        block = items_ref[lanes(i), :]
        numerator = numerator + jnp.dot(plan, block, preferred_element_type=f32)
        return numerator, mass + jnp.sum(plan.astype(f32), axis=1, keepdims=True)

    numerator, mass = over_pieces(
        gather_codes, (jnp.zeros((codes, features), f32), jnp.zeros((codes, 1), f32))
    )
    newc_ref[...] = numerator / mass

    start = (y * cores + core) * half + chip * rows
    def pick(i, total):
        lane = lax.broadcasted_iota(jnp.int32, (rows, width), 1) + i * width
        row = lax.broadcasted_iota(jnp.int32, (rows, width), 0) + start
        chosen = jnp.where(lane == row, u_ref[:, lanes(i)], 0.0)
        return total + jnp.sum(chosen, axis=1, keepdims=True)

    u_mine = over_pieces(pick, jnp.zeros((rows, 1), f32))

    drain(part_in.at[pl.ds(0, shards - 1)], part_recv)
    own = pl.ds(pl.multiple_of((core * line + chip) * rows, rows), rows)
    part_in[c] = part_out[own, :]
    rebuilt = jnp.zeros((rows, features), f32)
    if shards <= 32:
        for j in range(shards):
            rebuilt = rebuilt + part_in[j].astype(f32)
    else:
        rebuilt = lax.fori_loop(
            0, shards, lambda j, t: t + part_in[j].astype(f32), rebuilt
        )
    next_ref[...] = res_ref[...].astype(f32) - rebuilt * u_mine

    drain(items_ref.at[pl.ds(0, (chips - 1) * rows)], gather_send)
    if cores == 2:
        drain(items_ref.at[pl.ds(0, chips * rows)], pair_send)
    for sweep in range(ITERS):
        drain(row_in.at[sweep, pl.ds(0, shards - 1)], row_send.at[sweep])
    drain(part_in.at[pl.ds(0, shards - 1)], part_send)


def shards_of(groups, shards, residuals, codebook):
    rows, features = residuals.shape
    codes = codebook.shape[0]
    cores = 2 if shards % 2 == 0 else 1
    items = groups * shards * rows
    f32, bf16 = jnp.float32, jnp.bfloat16
    dma = pltpu.SemaphoreType.DMA
    vmem = pl.BlockSpec(memory_space=pltpu.VMEM)
    hbm = pl.BlockSpec(memory_space=pltpu.HBM)
    return pl.pallas_call(
        functools.partial(kernel, groups, shards, cores),
        out_shape=(
            jax.ShapeDtypeStruct((codes, features), f32),
            jax.ShapeDtypeStruct((rows, features), f32),
        ),
        in_specs=[hbm, hbm],
        out_specs=(vmem, vmem),
        scratch_shapes=[
            pltpu.VMEM((rows, features), bf16),
            pltpu.VMEM((codes, features), bf16),
            pltpu.VMEM((items, features), bf16),
            pltpu.VMEM((codes, items), f32),
            pltpu.VMEM((1, items), f32),
            pltpu.VMEM((ITERS, 1, items), f32),
            pltpu.VMEM((ITERS, shards, 1, items), f32),
            pltpu.VMEM((shards * rows, features), PART),
            pltpu.VMEM((shards, rows, features), PART),
            dma((2,)), dma, dma((groups,)), dma, dma, dma((ITERS,)), dma((ITERS,)), dma, dma,
        ],
        compiler_params=pltpu.CompilerParams(
            collective_id=0, has_side_effects=True, vmem_limit_bytes=48 * 2**20
        ),
    )(residuals, codebook)


def solution(mesh):
    groups, shards = mesh.shape["items"], mesh.shape["codes"]
    return jax.shard_map(
        functools.partial(shards_of, groups, shards),
        mesh=mesh,
        in_specs=(P(("items", "codes"), None), P("codes", None)),
        out_specs=(P("codes", None), P(("items", "codes"), None)),
        check_vma=False,
    )
```

```python
import functools
import math

import jax
import jax.numpy as jnp
from jax import lax
from jax.experimental import pallas as pl
from jax.experimental.pallas import tpu as pltpu
from jax.sharding import PartitionSpec as P

ITERS = 3
EPSILON = 1e-06
SHARPNESS = 40.0
PART = jnp.bfloat16
MESH = pl.DeviceIdType.MESH
NT = (((1,), (1,)), ((), ()))
TN = (((0,), (0,)), ((), ()))


def drain(ref, sem):
    pltpu.make_async_copy(ref, ref, sem).wait()


def each(count, body):
    if count <= 32:
        for i in range(count):
            body(i)
    else:
        pl.loop(0, count)(body)


def kernel(
    groups, shards, cores,
    res_hbm, code_hbm, newc_ref, next_ref,
    res_ref, code_ref, items_ref, kern_ref, u_ref, row_out, row_in, part_out, part_in,
    load, gather_send, gather_recv, pair_send, pair_recv, row_send, row_recv, part_send, part_recv,
):
    f32, bf16 = jnp.float32, jnp.bfloat16
    y, c = lax.axis_index("items"), lax.axis_index("codes")
    rows, features = res_ref.shape
    codes = code_ref.shape[0]
    devices = groups * shards
    items = devices * rows
    line = shards // cores
    half = line * rows
    core, chip = lax.rem(c, cores), lax.div(c, cores)

    def start_of(group, lane):
        return pl.multiple_of((group * cores + lane) * half, half)

    barrier = pltpu.get_barrier_semaphore()
    spot = y * line + chip
    chips = groups * line
    partners = chips - 1 + (line if cores == 2 else 0)

    def greet_chip(i):
        other = lax.rem(spot + i + 1, chips)
        pl.semaphore_signal(
            barrier, inc=1,
            device_id=(lax.div(other, line), lax.rem(other, line) * cores + core),
            device_id_type=MESH,
        )

    def greet_core(i):
        other = lax.rem(chip + i, line) * cores + 1 - core
        pl.semaphore_signal(barrier, inc=1, device_id=(y, other), device_id_type=MESH)

    each(chips - 1, greet_chip)
    if cores == 2:
        each(line, greet_core)
    load_res = pltpu.make_async_copy(res_hbm, res_ref, load.at[0])
    load_code = pltpu.make_async_copy(code_hbm, code_ref, load.at[1])
    load_res.start()
    load_code.start()

    load_res.wait()
    load_code.wait()
    mine = pl.ds(pl.multiple_of((y * cores + core) * half + chip * rows, rows), rows)
    items_ref[mine, :] = res_ref[...]
    code = code_ref[...]
    code32 = code.astype(f32)
    code_scale = lax.rsqrt(jnp.sum(code32 * code32, axis=1, keepdims=True) / features + EPSILON)
    code_scale = code_scale * (SHARPNESS * math.log2(math.e) / features)
    pl.semaphore_wait(barrier, partners)

    def spread(i):
        other = lax.rem(2 * chips - 1 - spot - i, chips)

        @pl.when(other != spot)
        def _():
            pltpu.make_async_remote_copy(
                src_ref=res_ref, dst_ref=items_ref.at[mine],
                send_sem=gather_send, recv_sem=gather_recv.at[y],
                device_id=(lax.div(other, line), lax.rem(other, line) * cores + core),
                device_id_type=MESH,
            ).start()

    each(chips, spread)
    for i in range(groups):
        g = lax.rem(y + i, groups)
        arrive = (line - 1 if i == 0 else line) * rows
        if arrive:
            drain(items_ref.at[pl.ds(0, arrive)], gather_recv.at[g])
        if cores == 2:
            block = items_ref.at[pl.ds(start_of(g, core), half)]
            pltpu.make_async_remote_copy(
                src_ref=block, dst_ref=block, send_sem=pair_send, recv_sem=pair_recv,
                device_id=(y, c + 1 - 2 * core), device_id_type=MESH,
            ).start()

    ones = jnp.ones((16, features), bf16)

    def build(start):
        block = items_ref[pl.ds(start, half), :]
        sim = lax.dot_general(code, block, NT, preferred_element_type=f32)
        wide = block.astype(f32)
        square = wide * wide
        high = square.astype(bf16)
        low = (square - high.astype(f32)).astype(bf16)
        mean = lax.dot_general(ones, high, NT, preferred_element_type=f32)
        mean = mean + lax.dot_general(ones, low, NT, preferred_element_type=f32)
        row_scale = lax.rsqrt(mean[0:1] / features + EPSILON)
        kern_ref[:, pl.ds(start, half)] = jnp.exp2(sim * code_scale * row_scale)

    each(groups, lambda g: build(start_of(g, core)))
    if cores == 2:
        drain(items_ref.at[pl.ds(0, chips * rows)], pair_recv)
        each(groups, lambda g: build(start_of(g, 1 - core)))

    width = math.gcd(items, 512)
    pieces = items // width

    def lanes(i):
        if pieces == 1:
            return pl.ds(0, width)
        return pl.ds(pl.multiple_of(i * width, width), width)

    def over_pieces(body, carry):
        if pieces == 1:
            return body(0, carry)
        return lax.fori_loop(0, pieces, body, carry)

    balance = items / (codes * shards)

    def column_sum(first):
        def body(i, total):
            k = kern_ref[:, lanes(i)]
            if not first:
                k = k * u_ref[:, lanes(i)]
            return total + jnp.sum(k, axis=1, keepdims=True)
        return over_pieces(body, jnp.zeros((codes, 1), f32))

    def row_sum(sweep, v):
        def body(i, none):
            row_out[sweep, :, lanes(i)] = jnp.sum(kern_ref[:, lanes(i)] * v, axis=0, keepdims=True)
            return none
        over_pieces(body, 0)

    def send_rows(sweep):
        def one(j):
            other = lax.rem(2 * shards - 1 - c - j, shards)

            @pl.when(other != c)
            def _():
                pltpu.make_async_remote_copy(
                    src_ref=row_out.at[sweep], dst_ref=row_in.at[sweep, c],
                    send_sem=row_send.at[sweep], recv_sem=row_recv.at[sweep],
                    device_id=(y, other), device_id_type=MESH,
                ).start()
        each(shards, one)

    def finish_rows(sweep):
        drain(row_in.at[sweep, pl.ds(0, shards - 1)], row_recv.at[sweep])
        row_in[sweep, c] = row_out[sweep]

        def body(i, none):
            total = jnp.zeros((1, width), f32)
            if shards <= 32:
                for j in range(shards):
                    total = total + row_in[sweep, j, :, lanes(i)]
            else:
                total = lax.fori_loop(
                    0, shards, lambda j, t: t + row_in[sweep, j, :, lanes(i)], total
                )
            u_ref[:, lanes(i)] = 1.0 / total
            return none
        over_pieces(body, 0)

    for sweep in range(ITERS):
        v = balance / column_sum(sweep == 0)
        row_sum(sweep, v)
        send_rows(sweep)
        if sweep < ITERS - 1:
            finish_rows(sweep)

    def scale(i, none):
        kern_ref[:, lanes(i)] = kern_ref[:, lanes(i)] * v
        return none

    over_pieces(scale, 0)

    def partial(lane):
        plan = kern_ref[:, pl.ds(start_of(y, lane), half)].astype(bf16)
        part = lax.dot_general(plan, code, TN, preferred_element_type=f32)
        part_out[pl.ds(lane * half, half), :] = part.astype(part_out.dtype)

    def send_part(lane, i):
        place = lax.rem(2 * line - 1 - chip - i, line)
        other = place * cores + lane

        @pl.when(other != c)
        def _():
            pltpu.make_async_remote_copy(
                src_ref=part_out.at[pl.ds(pl.multiple_of((lane * line + place) * rows, rows), rows)],
                dst_ref=part_in.at[c],
                send_sem=part_send, recv_sem=part_recv,
                device_id=(y, other), device_id_type=MESH,
            ).start()

    for lane in range(cores):
        partial(lane)
        each(line, functools.partial(send_part, lane))

    finish_rows(ITERS - 1)

    def gather_codes(i, carry):
        numerator, mass = carry
        plan = (kern_ref[:, lanes(i)] * u_ref[:, lanes(i)]).astype(bf16)
        block = items_ref[lanes(i), :]
        numerator = numerator + jnp.dot(plan, block, preferred_element_type=f32)
        return numerator, mass + jnp.sum(plan.astype(f32), axis=1, keepdims=True)

    numerator, mass = over_pieces(
        gather_codes, (jnp.zeros((codes, features), f32), jnp.zeros((codes, 1), f32))
    )
    newc_ref[...] = numerator / mass

    start = (y * cores + core) * half + chip * rows
    def pick(i, total):
        lane = lax.broadcasted_iota(jnp.int32, (rows, width), 1) + i * width
        row = lax.broadcasted_iota(jnp.int32, (rows, width), 0) + start
        chosen = jnp.where(lane == row, u_ref[:, lanes(i)], 0.0)
        return total + jnp.sum(chosen, axis=1, keepdims=True)

    u_mine = over_pieces(pick, jnp.zeros((rows, 1), f32))

    drain(part_in.at[pl.ds(0, shards - 1)], part_recv)
    own = pl.ds(pl.multiple_of((core * line + chip) * rows, rows), rows)
    part_in[c] = part_out[own, :]
    rebuilt = jnp.zeros((rows, features), f32)
    if shards <= 32:
        for j in range(shards):
            rebuilt = rebuilt + part_in[j].astype(f32)
    else:
        rebuilt = lax.fori_loop(
            0, shards, lambda j, t: t + part_in[j].astype(f32), rebuilt
        )
    next_ref[...] = res_ref[...].astype(f32) - rebuilt * u_mine

    drain(items_ref.at[pl.ds(0, (chips - 1) * rows)], gather_send)
    if cores == 2:
        drain(items_ref.at[pl.ds(0, chips * rows)], pair_send)
    for sweep in range(ITERS):
        drain(row_in.at[sweep, pl.ds(0, shards - 1)], row_send.at[sweep])
    drain(part_in.at[pl.ds(0, shards - 1)], part_send)


def shards_of(groups, shards, residuals, codebook):
    rows, features = residuals.shape
    codes = codebook.shape[0]
    cores = 2 if shards % 2 == 0 else 1
    items = groups * shards * rows
    f32, bf16 = jnp.float32, jnp.bfloat16
    dma = pltpu.SemaphoreType.DMA
    vmem = pl.BlockSpec(memory_space=pltpu.VMEM)
    hbm = pl.BlockSpec(memory_space=pltpu.HBM)
    return pl.pallas_call(
        functools.partial(kernel, groups, shards, cores),
        out_shape=(
            jax.ShapeDtypeStruct((codes, features), f32),
            jax.ShapeDtypeStruct((rows, features), f32),
        ),
        in_specs=[hbm, hbm],
        out_specs=(vmem, vmem),
        scratch_shapes=[
            pltpu.VMEM((rows, features), bf16),
            pltpu.VMEM((codes, features), bf16),
            pltpu.VMEM((items, features), bf16),
            pltpu.VMEM((codes, items), f32),
            pltpu.VMEM((1, items), f32),
            pltpu.VMEM((ITERS, 1, items), f32),
            pltpu.VMEM((ITERS, shards, 1, items), f32),
            pltpu.VMEM((shards * rows, features), PART),
            pltpu.VMEM((shards, rows, features), PART),
            dma((2,)), dma, dma((groups,)), dma, dma, dma((ITERS,)), dma((ITERS,)), dma, dma,
        ],
        compiler_params=pltpu.CompilerParams(
            collective_id=0, has_side_effects=True, vmem_limit_bytes=48 * 2**20
        ),
    )(residuals, codebook)


def solution(mesh):
    groups, shards = mesh.shape["items"], mesh.shape["codes"]
    return jax.shard_map(
        functools.partial(shards_of, groups, shards),
        mesh=mesh,
        in_specs=(P(("items", "codes"), None), P("codes", None)),
        out_specs=(P("codes", None), P(("items", "codes"), None)),
        check_vma=False,
    )
```
